512 devices in a mesh: atom: 32 (over z, core), kvec: 16 (over x, y).
Axes of the slice: x: 4, y: 4, z: 16, core: 2. Of those that a mesh axis runs over, the one named last changes fastest.
Arguments:
- features: float32 [49152, 256], P(('atom', 'kvec')), may hold values from -6 to 6
- fractions: int32 [3, 49152], P(None, 'atom'), may hold values from 0 to 1023
- wave_index: int32 [3, 8192], P(None, 'kvec'), may hold values from -12 to 12
- brick_count: int32 [32], replicated, may hold values from 1 to 1536, 24576 in all
- value_weight: float32 [256, 256], replicated, may hold values from -0.375 to 0.375
- k_filter: float32 [2, 8192, 256], P(None, 'kvec'), may hold values from -6 to 6
- mix_weight: float32 [2, 256, 256], replicated, may hold values from -0.25 to 0.25
- out_weight: float32 [256, 256], replicated, may hold values from -0.375 to 0.375
- norm_gain: float32 [256], replicated, may hold values from 0.5 to 1.5
- up_weight: float32 [256, 512], replicated, may hold values from -0.375 to 0.375
- down_weight: float32 [512, 256], replicated, may hold values from -0.25 to 0.25
Outputs:
- updated: float32 [49152, 256], P(('atom', 'kvec'))
The draws below stay inside these ranges and needn't reach their ends.
Inputs may be any that keep to these rules, and one draw needn't show every extreme that they name: Brick b holds its atoms in its first brick_count[b] slots; the counts sum to 24576 and the largest equals 1536.
All inputs are finite; a program needn't handle non-finite values.
Results may differ from the reference program's by a relative error of at most 0.0003.
Values sent between devices are 32-bit elements; how exact they have to be, the bound alone decides.
No kernel may reach another device: no remote copies, remote signals or barrier semaphores. Data moves between devices by JAX's collectives and lax.ppermute only.
A program may use at most 64 MiB of HBM per device.

```python
import math
import jax
import jax.numpy as jnp
import numpy as np
from jax import lax

W = 256
HID = 512
CAP = 1536
K = 8192
ATOMS_PAD = 49152
TOTAL = 24576
N_ATOM = 32


def touch_ends(result, key, low, high):
    spot = [jax.random.randint(jax.random.fold_in(key, axis), (), 0, length) for axis, length in enumerate(result.shape)]
    widest = result.shape.index(max(result.shape))
    next_to = spot[:widest] + [(spot[widest] + 1) % result.shape[widest]] + spot[widest + 1:]
    return result.at[tuple(spot)].set(low).at[tuple(next_to)].set(high)


def block_levels(stream_key, shape, cuts, low, largest):
    level, own = 1.0, jax.random.fold_in(stream_key, 6)
    for dim, parts in cuts:
        draws = jnp.exp(jax.random.uniform(jax.random.fold_in(own, dim), (parts,), jnp.float32, low / len(cuts), largest / len(cuts)))
        level = level * jnp.repeat(draws, shape[dim] // parts).reshape([-1 if axis == dim else 1 for axis in range(len(shape))])
    return level


def split_up(number_of, total, most, lean):
    portions = [(1 << 20) // math.isqrt(standing ** lean) + 1 for standing in range(2, number_of + 1)]
    rest, given = total - most - (number_of - 1), [1] * (number_of - 1)
    while rest > 0:
        movable = [i for i in range(number_of - 1) if given[i] < most]
        whole, budget = sum([portions[i] for i in movable]), rest
        for i in movable:
            addition = min(most - given[i], max(1, budget * portions[i] // whole), rest)
            given[i] = given[i] + addition
            rest = rest - addition
    return np.array([most] + given)


def ragged_sizes(rng, amount, total, bound, skew):
    if amount == 2:
        one = jax.random.randint(rng, (), max(1, total - bound), min(bound, total - 1) + 1)
        return jnp.stack([one, total - one])
    tallies = jnp.asarray(split_up(amount, total, bound, skew), jnp.int32)
    pairs = (amount - 1) // 2
    source_of, taker = tallies[1:1 + 2 * pairs:2], tallies[2:2 + 2 * pairs:2]
    room = jnp.minimum(source_of - 1, bound - taker)
    shifted = jax.random.randint(jax.random.fold_in(rng, 1), (pairs,), 0, 1 << 20) % (room + 1)
    tallies = tallies.at[1:1 + 2 * pairs:2].set(source_of - shifted).at[2:2 + 2 * pairs:2].set(taker + shifted)
    return tallies[jax.random.permutation(jax.random.fold_in(rng, 2), amount)]


def centred(rng, shape, deviation, limit, shards=(), kind=jnp.bfloat16):
    level = block_levels(rng, shape, shards, -0.22, 0.18) if shards else 1.0
    result = jax.random.normal(rng, shape, jnp.float32) * deviation * level
    return jnp.minimum(jnp.maximum(result, -limit), limit).astype(kind)


def setup_inputs(seed: int = 0) -> dict:
    streams_of = jax.random.split(jax.random.key(seed), 12)
    return {
        "features": centred(streams_of[0], (ATOMS_PAD, W), 1.0, 6.0, ((0, 512),), jnp.float32),
        "fractions": touch_ends(jax.random.randint(streams_of[1], (3, ATOMS_PAD), 0, 1024), jax.random.fold_in(streams_of[1], 1), 0, 1023).astype(jnp.int32),
        "wave_index": touch_ends(jax.random.randint(streams_of[2], (3, K), -12, 13), jax.random.fold_in(streams_of[2], 1), -12, 12).astype(jnp.int32),
        "brick_count": ragged_sizes(streams_of[3], N_ATOM, TOTAL, CAP, 2).astype(jnp.int32),
        "value_weight": centred(streams_of[4], (W, W), W ** -0.5, 0.375, (), jnp.float32),
        "k_filter": centred(streams_of[5], (2, K, W), 1.0, 6.0, ((1, 16),), jnp.float32),
        "mix_weight": centred(streams_of[6], (2, W, W), (2 * W) ** -0.5, 0.25, (), jnp.float32),
        "out_weight": centred(streams_of[7], (W, W), W ** -0.5, 0.375, (), jnp.float32),
        "norm_gain": jnp.clip(1.0 + 0.1 * jax.random.normal(streams_of[8], (W,), jnp.float32), 0.5, 1.5),
        "up_weight": centred(streams_of[9], (W, HID), W ** -0.5, 0.375, (), jnp.float32),
        "down_weight": centred(streams_of[10], (HID, W), HID ** -0.5, 0.25, (), jnp.float32),
    }


phase_step = 2.0 * math.pi / 1024.0
exact = lax.Precision.HIGHEST

def phases(frac_rows, wave_index):
    phase_index = frac_rows[0][:, None] * wave_index[0][None, :]
    phase_index = phase_index + frac_rows[1][:, None] * wave_index[1][None, :]
    phase_index = phase_index + frac_rows[2][:, None] * wave_index[2][None, :]
    angles = jnp.mod(phase_index, 1024).astype(jnp.float32) * phase_step
    return (jnp.cos(angles), jnp.sin(angles))

def mixing(real_part, imag_part, filt_real, filt_imag, mix_weight, normalizer):
    mixed_real = real_part * filt_real - imag_part * filt_imag
    mixed_imag = real_part * filt_imag + imag_part * filt_real
    out_real = (jnp.dot(mixed_real, mix_weight[0], precision=exact) - jnp.dot(mixed_imag, mix_weight[1], precision=exact)) * normalizer
    out_imag = (jnp.dot(mixed_real, mix_weight[1], precision=exact) + jnp.dot(mixed_imag, mix_weight[0], precision=exact)) * normalizer
    return (out_real, out_imag)

def reference(features, fractions, wave_index, brick_count, value_weight, k_filter, mix_weight, out_weight, norm_gain, up_weight, down_weight):
    slots = jnp.arange(CAP, dtype=jnp.int32)
    live_mask = (slots[None, :] < brick_count[:, None]).astype(jnp.float32).reshape(N_ATOM * CAP)
    values = jnp.dot(features, value_weight, precision=exact) * live_mask[:, None]
    brick_values = values.reshape(N_ATOM, CAP, W)
    brick_fracs = jnp.transpose(fractions.reshape(3, N_ATOM, CAP), (1, 0, 2))

    def collect(partial_value, item):
        value_rows, frac_rows = item
        cosine, sine_part = phases(frac_rows, wave_index)
        real_part = partial_value[0] + jnp.dot(cosine.T, value_rows, precision=exact)
        imag_part = partial_value[1] - jnp.dot(sine_part.T, value_rows, precision=exact)
        return ((real_part, imag_part), None)
    empty_sums = jnp.zeros((K, W), jnp.float32)
    (real_sf, imag_sf), unused = lax.scan(collect, (empty_sums, empty_sums), (brick_values, brick_fracs))
    normalizer = 1.0 / math.sqrt(TOTAL * K)
    filt_real, filt_imag = mixing(real_sf, imag_sf, k_filter[0], k_filter[1], mix_weight, normalizer)

    def project_back(frac_rows):
        cosine, sine_part = phases(frac_rows, wave_index)
        return jnp.dot(cosine, filt_real, precision=exact) - jnp.dot(sine_part, filt_imag, precision=exact)
    messages = lax.map(project_back, brick_fracs).reshape(N_ATOM * CAP, W)
    residual = features + jnp.dot(messages, out_weight, precision=exact)
    normed = residual * lax.rsqrt(lax.optimization_barrier(jnp.mean(residual * residual, axis=1, keepdims=True)) + 1e-06) * norm_gain
    hidden = jax.nn.silu(jnp.dot(normed, up_weight, precision=exact))
    return (residual + jnp.dot(hidden, down_weight, precision=exact)) * live_mask[:, None]
```

```python
import math

import jax
import jax.numpy as jnp
from jax import lax
from jax.sharding import PartitionSpec as P

exact = lax.Precision.HIGHEST
high = lax.Precision.HIGH

SIN_HALF = (3.1415926401307073, -5.167710083507923, 2.5500775232148563, -0.5982912856211671, 0.07765766030589402)
COS_HALF = (0.9999999532476085, -4.934792830619664, 4.058411352862771, -1.3318765680813944, 0.21968961109803095)


def horner(x, coefficients):
    total = jnp.float32(coefficients[-1])
    for c in coefficients[-2::-1]:
        total = total * x + jnp.float32(c)
    return total


def cos_sin(turns):
    r = turns - jnp.round(turns)
    x = r * r
    s = r * horner(x, SIN_HALF)
    c = horner(x, COS_HALF)
    twice = s + s
    return 1.0 - twice * s, twice * c


def shards(
    features,
    fractions,
    wave_index,
    brick_count,
    value_weight,
    k_filter,
    mix_weight,
    out_weight,
    norm_gain,
    up_weight,
    down_weight,
):
    share = features.shape[0]
    width = features.shape[1]
    groups = lax.axis_size("kvec")
    bricks = lax.axis_size("atom")
    rings = bricks // 2
    capacity = share * groups
    k_shard = wave_index.shape[1]
    k_half = k_shard // 2
    k_own = k_half // rings
    normalizer = 1.0 / math.sqrt(bricks * capacity // 2 * (k_shard * groups))
    own_brick = lax.axis_index("atom")
    own_group = lax.axis_index("kvec")
    core = own_brick % 2
    along_z = own_brick // 2
    same_core = [[2 * z + c for z in range(rings)] for c in range(2)]
    swap = [(i, i ^ 1) for i in range(bricks)]
    brick_live = jnp.sum(jnp.where(jnp.arange(bricks, dtype=jnp.int32) == own_brick, brick_count, 0))

    gathered = lax.all_to_all(
        jnp.broadcast_to(features[None], (groups, share, width)), "kvec", 0, 0, tiled=True
    ).reshape(capacity, width)

    fracs = fractions.astype(jnp.float32)
    waves = wave_index.astype(jnp.float32) * (1.0 / 1024.0)
    waves_own = lax.dynamic_slice_in_dim(waves, core * k_half, k_half, 1)
    waves_other = lax.dynamic_slice_in_dim(waves, (1 - core) * k_half, k_half, 1)

    def turns(w):
        return (
            fracs[0][:, None] * w[0][None, :]
            + fracs[1][:, None] * w[1][None, :]
            + fracs[2][:, None] * w[2][None, :]
        )

    cos_own, sin_own = cos_sin(turns(waves_own))
    cos_other, sin_other = cos_sin(turns(waves_other))
    out_mix = jnp.stack(
        [jnp.dot(mix_weight[0], out_weight, precision=exact), jnp.dot(mix_weight[1], out_weight, precision=exact)]
    )

    live = (jnp.arange(capacity, dtype=jnp.int32) < brick_live)[:, None]
    values = jnp.where(live, gathered, 0.0)
    contract = (((0,), (0,)), ((), ()))

    def factors(cosine, sine):
        return jnp.concatenate(
            [
                lax.dot_general(cosine, values, contract, precision=high),
                -lax.dot_general(sine, values, contract, precision=high),
            ],
            axis=1,
        )

    passed = lax.ppermute(factors(cos_other, sin_other), "atom", swap)
    summed = factors(cos_own, sin_own) + passed
    parts = lax.all_to_all(
        summed.reshape(rings, k_own, 2 * width), "atom", 0, 0, axis_index_groups=same_core, tiled=True
    )
    total = jnp.sum(parts, axis=0)
    real_sf = jnp.dot(total[:, :width], value_weight, precision=exact)
    imag_sf = jnp.dot(total[:, width:], value_weight, precision=exact)
    offset = core * k_half + along_z * k_own
    filt = lax.dynamic_slice_in_dim(k_filter, offset, k_own, 1)
    u_re = real_sf * filt[0] - imag_sf * filt[1]
    u_im = real_sf * filt[1] + imag_sf * filt[0]
    t_re = (jnp.dot(u_re, out_mix[0], precision=exact) - jnp.dot(u_im, out_mix[1], precision=exact)) * normalizer
    t_im = (jnp.dot(u_re, out_mix[1], precision=exact) + jnp.dot(u_im, out_mix[0], precision=exact)) * normalizer
    mixed = jnp.concatenate([t_re, t_im], axis=1)
    t_own = lax.all_to_all(
        jnp.broadcast_to(mixed[None], (rings, k_own, 2 * width)),
        "atom",
        0,
        0,
        axis_index_groups=same_core,
        tiled=True,
    ).reshape(k_half, 2 * width)
    t_other = lax.ppermute(t_own, "atom", swap)

    def back(cosine, sine, t):
        return jnp.dot(cosine, t[:, :width], precision=high) - jnp.dot(sine, t[:, width:], precision=high)

    messages = back(cos_own, sin_own, t_own) + back(cos_other, sin_other, t_other)
    arrived = lax.all_to_all(messages.reshape(groups, share, width), "kvec", 0, 0, tiled=True)
    residual = features + jnp.sum(arrived, axis=0)
    normed = residual * lax.rsqrt(jnp.mean(residual * residual, axis=1, keepdims=True) + 1e-06) * norm_gain
    hidden = jax.nn.silu(jnp.dot(normed, up_weight, precision=exact))
    slots = own_group * share + jnp.arange(share, dtype=jnp.int32)
    keep = (slots < brick_live).astype(jnp.float32)[:, None]
    return (residual + jnp.dot(hidden, down_weight, precision=exact)) * keep


def solution(mesh):
    return jax.shard_map(
        shards,
        mesh=mesh,
        in_specs=(
            P(("atom", "kvec"), None),
            P(None, "atom"),
            P(None, "kvec"),
            P(),
            P(),
            P(None, "kvec", None),
            P(),
            P(),
            P(),
            P(),
            P(),
        ),
        out_specs=P(("atom", "kvec"), None),
        check_vma=False,
    )
```

```python
import math

import jax
import jax.numpy as jnp
from jax import lax
from jax.sharding import Mesh
from jax.sharding import PartitionSpec as P

exact = lax.Precision.HIGHEST
high = lax.Precision.HIGH
NEAR = 4

SIN_HALF = (3.1415926401307073, -5.167710083507923, 2.5500775232148563, -0.5982912856211671, 0.07765766030589402)


def cos_turns(turns):
    r = turns - jnp.round(turns)
    x = r * r
    total = jnp.float32(SIN_HALF[-1])
    for c in SIN_HALF[-2::-1]:
        total = total * x + jnp.float32(c)
    s = r * total
    return 1.0 - (s + s) * s


def exchange(blocks, axes):
    return lax.all_to_all(blocks, axes, 0, 0, tiled=True)


def to_all(block, axes):
    peers = lax.axis_size(axes)
    return exchange(jnp.broadcast_to(block[None], (peers, *block.shape)), axes)


def swap_cores(block):
    return lax.ppermute(block, "core", [(0, 1), (1, 0)])


def shards(
    features,
    fractions,
    wave_index,
    brick_count,
    value_weight,
    k_filter,
    mix_weight,
    out_weight,
    norm_gain,
    up_weight,
    down_weight,
):
    share, width = features.shape
    groups = lax.axis_size("kvec")
    far, near = lax.axis_size("far"), lax.axis_size("near")
    rings = far * near
    capacity = share * groups
    k_shard = wave_index.shape[1]
    k_half = k_shard // 2
    k_own = k_half // rings
    rows = 2 * k_own
    normalizer = 1.0 / math.sqrt(rings * capacity * (k_shard * groups))
    core = lax.axis_index("core")
    own_group = lax.axis_index("kvec")
    own_brick = (lax.axis_index("far") * near + lax.axis_index("near")) * 2 + core
    count = lax.dynamic_index_in_dim(brick_count, own_brick, 0, False)

    values = to_all(features, "kvec").reshape(capacity, width)

    live = (jnp.arange(capacity, dtype=jnp.int32) < count).astype(jnp.float32)
    fracs = fractions.astype(jnp.float32)
    waves = wave_index.astype(jnp.float32) * (1.0 / 1024.0)
    quarter = jnp.broadcast_to(jnp.array([0.0, 0.25], jnp.float32)[None, :, None], (rings, 2, k_own)).reshape(-1)

    def lines(which):
        w = lax.dynamic_slice_in_dim(waves, which * k_half, k_half, 1).reshape(3, rings, 1, k_own)
        return jnp.broadcast_to(w, (3, rings, 2, k_own)).reshape(3, 2 * k_half)

    def basis(w):
        turns = sum(fracs[j][:, None] * w[j][None, :] for j in range(3)) + quarter[None, :]
        return cos_turns(turns) * live[:, None]

    def basis_t(w):
        turns = sum(w[j][:, None] * fracs[j][None, :] for j in range(3)) + quarter[:, None]
        return cos_turns(turns) * live[None, :]

    w_own, w_other = lines(core), lines(1 - core)
    own, other, own_t, other_t = lax.optimization_barrier(
        (basis(w_own), basis(w_other), basis_t(w_own), basis_t(w_other))
    )
    out_mix = jnp.stack(
        [jnp.dot(mix_weight[0], out_weight, precision=exact), jnp.dot(mix_weight[1], out_weight, precision=exact)]
    )

    passed = swap_cores(jnp.dot(other_t, values, precision=high))
    summed = lax.optimization_barrier(jnp.dot(own_t, values, precision=high)) + passed
    close = jnp.sum(exchange(summed.reshape(near, far * rows, width), "near"), axis=0)
    raw = jnp.sum(lax.all_gather(close, "far", axis=0), axis=0)
    total = jnp.dot(raw, value_weight, precision=exact).reshape(far, 2, k_own, width)
    real_sf, imag_sf = total[:, 0], total[:, 1]
    kept = far * k_own
    filt = lax.dynamic_slice_in_dim(k_filter, core * k_half + lax.axis_index("near") * kept, kept, 1) * normalizer
    filt = filt.reshape(2, far, k_own, width)
    u_re = real_sf * filt[0] - imag_sf * filt[1]
    u_im = real_sf * filt[1] + imag_sf * filt[0]
    mixed = jnp.dot(jnp.stack([u_re, u_im], axis=1).reshape(far * rows, width), out_mix[0], precision=exact) + jnp.dot(
        jnp.stack([-u_im, u_re], axis=1).reshape(far * rows, width), out_mix[1], precision=exact
    )

    t_own = to_all(mixed, "near").reshape(rings * rows, width)
    t_other = swap_cores(t_own)
    messages = jnp.dot(own, t_own, precision=high) + jnp.dot(other, t_other, precision=high)
    landed = exchange(messages.reshape(groups, share, width), "kvec")
    residual = features + jnp.sum(landed, axis=0)
    normed = residual * lax.rsqrt(jnp.mean(residual * residual, axis=1, keepdims=True) + 1e-06) * norm_gain
    hidden = jax.nn.silu(jnp.dot(normed, up_weight, precision=exact))
    slots = own_group * share + jnp.arange(share, dtype=jnp.int32)
    keep = (slots < count).astype(jnp.float32)[:, None]
    return (residual + jnp.dot(hidden, down_weight, precision=exact)) * keep


def solution(mesh):
    bricks, groups = mesh.shape["atom"], mesh.shape["kvec"]
    grid = Mesh(
        mesh.devices.reshape(bricks // 2 // NEAR, NEAR, 2, groups), ("far", "near", "core", "kvec")
    )
    atom = ("far", "near", "core")
    return jax.shard_map(
        shards,
        mesh=grid,
        in_specs=(
            P((*atom, "kvec"), None),
            P(None, atom),
            P(None, "kvec"),
            P(),
            P(),
            P(None, "kvec", None),
            P(),
            P(),
            P(),
            P(),
            P(),
        ),
        out_specs=P((*atom, "kvec"), None),
        check_vma=False,
    )
```

```python
import math

import jax
import jax.numpy as jnp
from jax import lax
from jax.sharding import Mesh
from jax.sharding import PartitionSpec as P

exact = lax.Precision.HIGHEST
high = lax.Precision.HIGH
NEAR = 4
SIDE = 4
PLANE = [[i * SIDE + (i + d) % SIDE for d in range(SIDE) for i in range(SIDE)]]
LOOP = [[0, 1, 3, 2]]

SIN_HALF = (3.1415926401307073, -5.167710083507923, 2.5500775232148563, -0.5982912856211671, 0.07765766030589402)


def cos_turns(turns):
    r = turns - jnp.round(turns)
    x = r * r
    total = jnp.float32(SIN_HALF[-1])
    for c in SIN_HALF[-2::-1]:
        total = total * x + jnp.float32(c)
    s = r * total
    return 1.0 - (s + s) * s


def exchange(blocks, axes, sets=None):
    return lax.all_to_all(blocks, axes, 0, 0, axis_index_groups=sets, tiled=True)


def to_all(block, axes, sets=None):
    peers = lax.axis_size(axes)
    return exchange(jnp.broadcast_to(block[None], (peers, *block.shape)), axes, sets)


def swap_cores(block):
    return lax.ppermute(block, "core", [(0, 1), (1, 0)])


def shards(
    features,
    fractions,
    wave_index,
    brick_count,
    value_weight,
    k_filter,
    mix_weight,
    out_weight,
    norm_gain,
    up_weight,
    down_weight,
):
    share, width = features.shape
    groups = lax.axis_size("kvec")
    far, near = lax.axis_size("far"), lax.axis_size("near")
    rings = far * near
    capacity = share * groups
    k_shard = wave_index.shape[1]
    k_half = k_shard // 2
    k_own = k_half // rings
    rows = 2 * k_own
    normalizer = 1.0 / math.sqrt(rings * capacity * (k_shard * groups))
    core = lax.axis_index("core")
    own_group = lax.axis_index("kvec")
    own_brick = (lax.axis_index("far") * near + lax.axis_index("near")) * 2 + core
    count = lax.dynamic_index_in_dim(brick_count, own_brick, 0, False)

    values = to_all(features, "kvec", PLANE).reshape(capacity, width)

    def in_order(slots):
        return jnp.concatenate([slots[..., g * share : (g + 1) * share] for g in PLANE[0]], axis=-1)

    live = in_order((jnp.arange(capacity, dtype=jnp.int32) < count).astype(jnp.float32))
    fracs = in_order(fractions.astype(jnp.float32))
    waves = wave_index.astype(jnp.float32) * (1.0 / 1024.0)
    quarter = jnp.broadcast_to(jnp.array([0.0, 0.25], jnp.float32)[None, :, None], (rings, 2, k_own)).reshape(-1)

    def lines(which):
        w = lax.dynamic_slice_in_dim(waves, which * k_half, k_half, 1).reshape(3, rings, 1, k_own)
        return jnp.broadcast_to(w, (3, rings, 2, k_own)).reshape(3, 2 * k_half)

    def basis(w):
        turns = sum(fracs[j][:, None] * w[j][None, :] for j in range(3)) + quarter[None, :]
        return cos_turns(turns) * live[:, None]

    def basis_t(w):
        turns = sum(w[j][:, None] * fracs[j][None, :] for j in range(3)) + quarter[:, None]
        return cos_turns(turns) * live[None, :]

    def looped(w):
        return jnp.concatenate([jnp.split(w, near, axis=1)[n] for n in LOOP[0]], axis=1)

    w_own, w_other = lines(core), lines(1 - core)
    own, other, own_t, other_t = lax.optimization_barrier(
        (basis(w_own), basis(w_other), basis_t(looped(w_own)), basis_t(looped(w_other)))
    )
    out_mix = jnp.stack(
        [jnp.dot(mix_weight[0], out_weight, precision=exact), jnp.dot(mix_weight[1], out_weight, precision=exact)]
    )

    passed = swap_cores(jnp.dot(other_t, values, precision=high))
    summed = lax.optimization_barrier(jnp.dot(own_t, values, precision=high)) + passed
    close = jnp.sum(exchange(summed.reshape(near, far * rows, width), "near", LOOP), axis=0)
    raw = jnp.sum(lax.all_gather(close, "far", axis=0), axis=0)
    total = jnp.dot(raw, value_weight, precision=exact).reshape(far, 2, k_own, width)
    real_sf, imag_sf = total[:, 0], total[:, 1]
    kept = far * k_own
    filt = lax.dynamic_slice_in_dim(k_filter, core * k_half + lax.axis_index("near") * kept, kept, 1) * normalizer
    filt = filt.reshape(2, far, k_own, width)
    u_re = real_sf * filt[0] - imag_sf * filt[1]
    u_im = real_sf * filt[1] + imag_sf * filt[0]
    mixed = jnp.dot(jnp.stack([u_re, u_im], axis=1).reshape(far * rows, width), out_mix[0], precision=exact) + jnp.dot(
        jnp.stack([-u_im, u_re], axis=1).reshape(far * rows, width), out_mix[1], precision=exact
    )

    t_own = lax.all_gather(mixed, "near", axis=0, tiled=True)
    t_other = swap_cores(t_own)
    messages = jnp.dot(own, t_own, precision=high) + jnp.dot(other, t_other, precision=high)
    landed = exchange(messages.reshape(groups, share, width), "kvec", PLANE)
    residual = features + jnp.sum(landed, axis=0)
    normed = residual * lax.rsqrt(jnp.mean(residual * residual, axis=1, keepdims=True) + 1e-06) * norm_gain
    hidden = jax.nn.silu(jnp.dot(normed, up_weight, precision=exact))
    slots = own_group * share + jnp.arange(share, dtype=jnp.int32)
    keep = (slots < count).astype(jnp.float32)[:, None]
    return (residual + jnp.dot(hidden, down_weight, precision=exact)) * keep


def solution(mesh):
    bricks, groups = mesh.shape["atom"], mesh.shape["kvec"]
    grid = Mesh(
        mesh.devices.reshape(bricks // 2 // NEAR, NEAR, 2, groups), ("far", "near", "core", "kvec")
    )
    atom = ("far", "near", "core")
    return jax.shard_map(
        shards,
        mesh=grid,
        in_specs=(
            P((*atom, "kvec"), None),
            P(None, atom),
            P(None, "kvec"),
            P(),
            P(),
            P(None, "kvec", None),
            P(),
            P(),
            P(),
            P(),
            P(),
        ),
        out_specs=P((*atom, "kvec"), None),
        check_vma=False,
    )
```

```python
import math

import jax
import jax.numpy as jnp
from jax import lax
from jax.sharding import Mesh
from jax.sharding import PartitionSpec as P

exact = lax.Precision.HIGHEST
high = lax.Precision.HIGH
NEAR = 4
SIDE = 4
PLANE = [[i * SIDE + (i + d) % SIDE for d in range(SIDE) for i in range(SIDE)]]
LOOP = [[0, 1, 3, 2]]

SIN_HALF = (3.1415926401307073, -5.167710083507923, 2.5500775232148563, -0.5982912856211671, 0.07765766030589402)


def cos_turns(turns):
    r = turns - jnp.round(turns)
    x = r * r
    total = jnp.float32(SIN_HALF[-1])
    for c in SIN_HALF[-2::-1]:
        total = total * x + jnp.float32(c)
    s = r * total
    return 1.0 - (s + s) * s


def exchange(blocks, axes, sets=None):
    return lax.all_to_all(blocks, axes, 0, 0, axis_index_groups=sets, tiled=True)


def to_all(block, axes, sets=None):
    peers = lax.axis_size(axes)
    return exchange(jnp.broadcast_to(block[None], (peers, *block.shape)), axes, sets)


def swap_cores(block):
    return lax.ppermute(block, "core", [(0, 1), (1, 0)])


def shards(
    features,
    fractions,
    wave_index,
    brick_count,
    value_weight,
    k_filter,
    mix_weight,
    out_weight,
    norm_gain,
    up_weight,
    down_weight,
):
    share, width = features.shape
    groups = lax.axis_size("kvec")
    far, near = lax.axis_size("far"), lax.axis_size("near")
    rings = far * near
    capacity = share * groups
    k_shard = wave_index.shape[1]
    k_half = k_shard // 2
    k_own = k_half // rings
    rows = 2 * k_own
    normalizer = 1.0 / math.sqrt(rings * capacity * (k_shard * groups))
    core = lax.axis_index("core")
    own_group = lax.axis_index("kvec")
    own_brick = (lax.axis_index("far") * near + lax.axis_index("near")) * 2 + core
    count = lax.dynamic_index_in_dim(brick_count, own_brick, 0, False)

    values = to_all(features, "kvec", PLANE).reshape(capacity, width)

    def in_order(slots):
        return jnp.concatenate([slots[..., g * share : (g + 1) * share] for g in PLANE[0]], axis=-1)

    live = in_order((jnp.arange(capacity, dtype=jnp.int32) < count).astype(jnp.float32))
    fracs = in_order(fractions.astype(jnp.float32))
    waves = wave_index.astype(jnp.float32) * (1.0 / 1024.0)
    quarter = jnp.broadcast_to(jnp.array([0.0, 0.25], jnp.float32)[None, :, None], (rings, 2, k_own)).reshape(-1)

    def lines(which):
        w = lax.dynamic_slice_in_dim(waves, which * k_half, k_half, 1).reshape(3, rings, 1, k_own)
        return jnp.broadcast_to(w, (3, rings, 2, k_own)).reshape(3, 2 * k_half)

    def basis(w):
        turns = sum(fracs[j][:, None] * w[j][None, :] for j in range(3)) + quarter[None, :]
        return cos_turns(turns) * live[:, None]

    def basis_t(w, slots):
        turns = sum(w[j][:, None] * fracs[j][None, slots] for j in range(3)) + quarter[:, None]
        return cos_turns(turns) * live[None, slots]

    def looped(w):
        return jnp.concatenate([jnp.split(w, near, axis=1)[n] for n in LOOP[0]], axis=1)

    w_own, w_other = lines(core), lines(1 - core)
    parts = [slice(0, capacity // 2), slice(capacity // 2, capacity)]
    own, other, own_t, other_t = lax.optimization_barrier(
        (
            basis(w_own),
            basis(w_other),
            basis_t(looped(w_own), slice(0, capacity)),
            [basis_t(looped(w_other), part) for part in parts],
        )
    )
    out_mix = jnp.stack(
        [jnp.dot(mix_weight[0], out_weight, precision=exact), jnp.dot(mix_weight[1], out_weight, precision=exact)]
    )

    passed = swap_cores(
        sum(jnp.dot(basis_part, values[part], precision=high) for basis_part, part in zip(other_t, parts))
    )
    summed = lax.optimization_barrier(jnp.dot(own_t, values, precision=high)) + passed
    close = jnp.sum(exchange(summed.reshape(near, far * rows, width), "near", LOOP), axis=0)
    raw = jnp.sum(lax.all_gather(close, "far", axis=0), axis=0)
    total = jnp.dot(raw, value_weight, precision=high).reshape(far, 2, k_own, width)
    real_sf, imag_sf = total[:, 0], total[:, 1]
    kept = far * k_own
    filt = lax.dynamic_slice_in_dim(k_filter, core * k_half + lax.axis_index("near") * kept, kept, 1) * normalizer
    filt = filt.reshape(2, far, k_own, width)
    u_re = real_sf * filt[0] - imag_sf * filt[1]
    u_im = real_sf * filt[1] + imag_sf * filt[0]
    mixed = jnp.dot(jnp.stack([u_re, u_im], axis=1).reshape(far * rows, width), out_mix[0], precision=high) + jnp.dot(
        jnp.stack([-u_im, u_re], axis=1).reshape(far * rows, width), out_mix[1], precision=high
    )

    t_own = lax.all_gather(mixed, "near", axis=0, tiled=True)
    t_other = swap_cores(t_own)
    messages = jnp.dot(own, t_own, precision=high) + jnp.dot(other, t_other, precision=high)
    landed = exchange(messages.reshape(groups, share, width), "kvec", PLANE)
    residual = features + jnp.sum(landed, axis=0)
    normed = residual * lax.rsqrt(jnp.mean(residual * residual, axis=1, keepdims=True) + 1e-06) * norm_gain
    hidden = jax.nn.silu(jnp.dot(normed, up_weight, precision=high))
    slots = own_group * share + jnp.arange(share, dtype=jnp.int32)
    keep = (slots < count).astype(jnp.float32)[:, None]
    return (residual + jnp.dot(hidden, down_weight, precision=high)) * keep


def solution(mesh):
    bricks, groups = mesh.shape["atom"], mesh.shape["kvec"]
    grid = Mesh(
        mesh.devices.reshape(bricks // 2 // NEAR, NEAR, 2, groups), ("far", "near", "core", "kvec")
    )
    atom = ("far", "near", "core")
    return jax.shard_map(
        shards,
        mesh=grid,
        in_specs=(
            P((*atom, "kvec"), None),
            P(None, atom),
            P(None, "kvec"),
            P(),
            P(),
            P(None, "kvec", None),
            P(),
            P(),
            P(),
            P(),
            P(),
        ),
        out_specs=P((*atom, "kvec"), None),
        check_vma=False,
    )
```

```python
import math

import jax
import jax.numpy as jnp
from jax import lax
from jax.sharding import Mesh
from jax.sharding import PartitionSpec as P

exact = lax.Precision.HIGHEST
high = lax.Precision.HIGH
NEAR = 4
SIDE = 4
PLANE = [[i * SIDE + (i + d) % SIDE for d in range(SIDE) for i in range(SIDE)]]
LOOP = [[0, 1, 3, 2]]

SIN_HALF = (3.1415926401307073, -5.167710083507923, 2.5500775232148563, -0.5982912856211671, 0.07765766030589402)


def cos_turns(turns):
    r = turns - jnp.round(turns)
    x = r * r
    total = jnp.float32(SIN_HALF[-1])
    for c in SIN_HALF[-2::-1]:
        total = total * x + jnp.float32(c)
    s = r * total
    return 1.0 - (s + s) * s


def exchange(blocks, axes, sets=None):
    return lax.all_to_all(blocks, axes, 0, 0, axis_index_groups=sets, tiled=True)


def to_all(block, axes, sets=None):
    peers = lax.axis_size(axes)
    return exchange(jnp.broadcast_to(block[None], (peers, *block.shape)), axes, sets)


def swap_cores(block):
    return lax.ppermute(block, "core", [(0, 1), (1, 0)])


def shards(
    features,
    fractions,
    wave_index,
    brick_count,
    value_weight,
    k_filter,
    mix_weight,
    out_weight,
    norm_gain,
    up_weight,
    down_weight,
):
    share, width = features.shape
    groups = lax.axis_size("kvec")
    far, near = lax.axis_size("far"), lax.axis_size("near")
    rings = far * near
    capacity = share * groups
    k_shard = wave_index.shape[1]
    k_half = k_shard // 2
    k_own = k_half // rings
    rows = 2 * k_own
    normalizer = 1.0 / math.sqrt(rings * capacity * (k_shard * groups))
    core = lax.axis_index("core")
    own_group = lax.axis_index("kvec")
    own_brick = (lax.axis_index("far") * near + lax.axis_index("near")) * 2 + core
    count = lax.dynamic_index_in_dim(brick_count, own_brick, 0, False)

    values = to_all(features, "kvec", PLANE).reshape(capacity, width)

    def in_order(slots):
        return jnp.concatenate([slots[..., g * share : (g + 1) * share] for g in PLANE[0]], axis=-1)

    live = in_order((jnp.arange(capacity, dtype=jnp.int32) < count).astype(jnp.float32))
    fracs = in_order(fractions.astype(jnp.float32))
    waves = wave_index.astype(jnp.float32) * (1.0 / 1024.0)
    quarter = jnp.broadcast_to(jnp.array([0.0, 0.25], jnp.float32)[None, :, None], (rings, 2, k_own)).reshape(-1)

    def lines(which):
        w = lax.dynamic_slice_in_dim(waves, which * k_half, k_half, 1).reshape(3, rings, 1, k_own)
        return jnp.broadcast_to(w, (3, rings, 2, k_own)).reshape(3, 2 * k_half)

    def basis(w):
        turns = sum(fracs[j][:, None] * w[j][None, :] for j in range(3)) + quarter[None, :]
        return cos_turns(turns) * live[:, None]

    def basis_t(w, slots):
        turns = sum(w[j][:, None] * fracs[j][None, slots] for j in range(3)) + quarter[:, None]
        return cos_turns(turns) * live[None, slots]

    def looped(w):
        return jnp.concatenate([jnp.split(w, near, axis=1)[n] for n in LOOP[0]], axis=1)

    w_own, w_other = lines(core), lines(1 - core)
    parts = [slice(0, capacity // 2), slice(capacity // 2, capacity)]
    own_t, other_t = lax.optimization_barrier(
        (
            basis_t(looped(w_own), slice(0, capacity)),
            [basis_t(looped(w_other), part) for part in parts],
        )
    )
    out_mix = jnp.stack(
        [jnp.dot(mix_weight[0], out_weight, precision=exact), jnp.dot(mix_weight[1], out_weight, precision=exact)]
    )

    passed = swap_cores(
        sum(jnp.dot(basis_part, values[part], precision=high) for basis_part, part in zip(other_t, parts))
    )
    summed = lax.optimization_barrier(jnp.dot(own_t, values, precision=high)) + passed
    summed, w_own, w_other = lax.optimization_barrier((summed, w_own, w_other))
    close = jnp.sum(exchange(summed.reshape(near, far * rows, width), "near", LOOP), axis=0)
    close, own, other = lax.optimization_barrier((close, basis(w_own), basis(w_other)))
    raw = jnp.sum(lax.all_gather(close, "far", axis=0), axis=0)
    total = jnp.dot(raw, value_weight, precision=high).reshape(far, 2, k_own, width)
    real_sf, imag_sf = total[:, 0], total[:, 1]
    kept = far * k_own
    filt = lax.dynamic_slice_in_dim(k_filter, core * k_half + lax.axis_index("near") * kept, kept, 1) * normalizer
    filt = filt.reshape(2, far, k_own, width)
    u_re = real_sf * filt[0] - imag_sf * filt[1]
    u_im = real_sf * filt[1] + imag_sf * filt[0]
    mixed = jnp.dot(jnp.stack([u_re, u_im], axis=1).reshape(far * rows, width), out_mix[0], precision=high) + jnp.dot(
        jnp.stack([-u_im, u_re], axis=1).reshape(far * rows, width), out_mix[1], precision=high
    )

    t_own = lax.all_gather(mixed, "near", axis=0, tiled=True)
    t_other = swap_cores(t_own)
    messages = jnp.dot(own, t_own, precision=high) + jnp.dot(other, t_other, precision=high)
    landed = exchange(messages.reshape(groups, share, width), "kvec", PLANE)
    residual = features + jnp.sum(landed, axis=0)
    normed = residual * lax.rsqrt(jnp.mean(residual * residual, axis=1, keepdims=True) + 1e-06) * norm_gain
    hidden = jax.nn.silu(jnp.dot(normed, up_weight, precision=high))
    slots = own_group * share + jnp.arange(share, dtype=jnp.int32)
    keep = (slots < count).astype(jnp.float32)[:, None]
    return (residual + jnp.dot(hidden, down_weight, precision=high)) * keep


def solution(mesh):
    bricks, groups = mesh.shape["atom"], mesh.shape["kvec"]
    grid = Mesh(
        mesh.devices.reshape(bricks // 2 // NEAR, NEAR, 2, groups), ("far", "near", "core", "kvec")
    )
    atom = ("far", "near", "core")
    return jax.shard_map(
        shards,
        mesh=grid,
        in_specs=(
            P((*atom, "kvec"), None),
            P(None, atom),
            P(None, "kvec"),
            P(),
            P(),
            P(None, "kvec", None),
            P(),
            P(),
            P(),
            P(),
            P(),
        ),
        out_specs=P((*atom, "kvec"), None),
        check_vma=False,
    )
```

```python
import math

import jax
import jax.numpy as jnp
from jax import lax
from jax.sharding import Mesh
from jax.sharding import PartitionSpec as P

exact = lax.Precision.HIGHEST
high = lax.Precision.HIGH
NEAR = 4
SIDE = 4
PLANE = [[i * SIDE + (i + d) % SIDE for d in range(SIDE) for i in range(SIDE)]]
LOOP = [[0, 1, 3, 2]]

SIN_HALF = (3.1415926401307073, -5.167710083507923, 2.5500775232148563, -0.5982912856211671, 0.07765766030589402)


def cos_turns(turns):
    r = turns - jnp.round(turns)
    x = r * r
    total = jnp.float32(SIN_HALF[-1])
    for c in SIN_HALF[-2::-1]:
        total = total * x + jnp.float32(c)
    s = r * total
    return 1.0 - (s + s) * s


def exchange(blocks, axes, sets=None):
    return lax.all_to_all(blocks, axes, 0, 0, axis_index_groups=sets, tiled=True)


def to_all(block, axes, sets=None):
    peers = lax.axis_size(axes)
    return exchange(jnp.broadcast_to(block[None], (peers, *block.shape)), axes, sets)


def swap_cores(block):
    return lax.ppermute(block, "core", [(0, 1), (1, 0)])


def shards(
    features,
    fractions,
    wave_index,
    brick_count,
    value_weight,
    k_filter,
    mix_weight,
    out_weight,
    norm_gain,
    up_weight,
    down_weight,
):
    share, width = features.shape
    groups = lax.axis_size("kvec")
    far, near = lax.axis_size("far"), lax.axis_size("near")
    rings = far * near
    capacity = share * groups
    k_shard = wave_index.shape[1]
    k_half = k_shard // 2
    k_own = k_half // rings
    rows = 2 * k_own
    normalizer = 1.0 / math.sqrt(rings * capacity * (k_shard * groups))
    core = lax.axis_index("core")
    own_group = lax.axis_index("kvec")
    own_brick = (lax.axis_index("far") * near + lax.axis_index("near")) * 2 + core
    count = lax.dynamic_index_in_dim(brick_count, own_brick, 0, False)

    values = to_all(features, "kvec", PLANE).reshape(capacity, width)

    def in_order(slots):
        return jnp.concatenate([slots[..., g * share : (g + 1) * share] for g in PLANE[0]], axis=-1)

    live = in_order((jnp.arange(capacity, dtype=jnp.int32) < count).astype(jnp.float32))
    fracs = in_order(fractions.astype(jnp.float32))
    waves = wave_index.astype(jnp.float32) * (1.0 / 1024.0)
    quarter = jnp.broadcast_to(jnp.array([0.0, 0.25], jnp.float32)[None, :, None], (rings, 2, k_own)).reshape(-1)

    def lines(which):
        w = lax.dynamic_slice_in_dim(waves, which * k_half, k_half, 1).reshape(3, rings, 1, k_own)
        return jnp.broadcast_to(w, (3, rings, 2, k_own)).reshape(3, 2 * k_half)

    def basis(w):
        turns = sum(fracs[j][:, None] * w[j][None, :] for j in range(3)) + quarter[None, :]
        return cos_turns(turns) * live[:, None]

    def basis_t(w, slots):
        turns = sum(w[j][:, None] * fracs[j][None, slots] for j in range(3)) + quarter[:, None]
        return cos_turns(turns) * live[None, slots]

    def looped(w):
        return jnp.concatenate([jnp.split(w, near, axis=1)[n] for n in LOOP[0]], axis=1)

    w_own, w_other = lines(core), lines(1 - core)
    parts = [slice(0, capacity // 3), slice(capacity // 3, capacity)]
    own_t, other_t = lax.optimization_barrier(
        (
            basis_t(looped(w_own), slice(0, capacity)),
            [basis_t(looped(w_other), part) for part in parts],
        )
    )
    out_mix = jnp.stack(
        [jnp.dot(mix_weight[0], out_weight, precision=exact), jnp.dot(mix_weight[1], out_weight, precision=exact)]
    )

    passed = swap_cores(
        sum(jnp.dot(basis_part, values[part], precision=high) for basis_part, part in zip(other_t, parts))
    )
    summed = lax.optimization_barrier(jnp.dot(own_t, values, precision=high)) + passed
    summed, w_own, w_other = lax.optimization_barrier((summed, w_own, w_other))
    close = jnp.sum(exchange(summed.reshape(near, far * rows, width), "near", LOOP), axis=0)
    close, own, other = lax.optimization_barrier((close, basis(w_own), basis(w_other)))
    raw = jnp.sum(lax.all_gather(close, "far", axis=0), axis=0)
    total = jnp.dot(raw, value_weight, precision=high).reshape(far, 2, k_own, width)
    real_sf, imag_sf = total[:, 0], total[:, 1]
    kept = far * k_own
    filt = lax.dynamic_slice_in_dim(k_filter, core * k_half + lax.axis_index("near") * kept, kept, 1) * normalizer
    filt = filt.reshape(2, far, k_own, width)
    u_re = real_sf * filt[0] - imag_sf * filt[1]
    u_im = real_sf * filt[1] + imag_sf * filt[0]
    mixed = jnp.dot(jnp.stack([u_re, u_im], axis=1).reshape(far * rows, width), out_mix[0], precision=high) + jnp.dot(
        jnp.stack([-u_im, u_re], axis=1).reshape(far * rows, width), out_mix[1], precision=high
    )

    t_own = lax.all_gather(mixed, "near", axis=0, tiled=True)
    t_other = swap_cores(t_own)
    messages = jnp.dot(own, t_own, precision=high) + jnp.dot(other, t_other, precision=high)
    landed = exchange(messages.reshape(groups, share, width), "kvec", PLANE)
    residual = features + jnp.sum(landed, axis=0)
    normed = residual * lax.rsqrt(jnp.mean(residual * residual, axis=1, keepdims=True) + 1e-06) * norm_gain
    hidden = jax.nn.silu(jnp.dot(normed, up_weight, precision=high))
    slots = own_group * share + jnp.arange(share, dtype=jnp.int32)
    keep = (slots < count).astype(jnp.float32)[:, None]
    return (residual + jnp.dot(hidden, down_weight, precision=high)) * keep


def solution(mesh):
    bricks, groups = mesh.shape["atom"], mesh.shape["kvec"]
    grid = Mesh(
        mesh.devices.reshape(bricks // 2 // NEAR, NEAR, 2, groups), ("far", "near", "core", "kvec")
    )
    atom = ("far", "near", "core")
    return jax.shard_map(
        shards,
        mesh=grid,
        in_specs=(
            P((*atom, "kvec"), None),
            P(None, atom),
            P(None, "kvec"),
            P(),
            P(),
            P(None, "kvec", None),
            P(),
            P(),
            P(),
            P(),
            P(),
        ),
        out_specs=P((*atom, "kvec"), None),
        check_vma=False,
    )
```
